512 devices in a mesh: grid: 16 (over x, y_lo), orb: 32 (over y_hi, z, core).
Axes of the slice: x: 4, y: 8 (y_hi: 2, y_lo: 4; y = y_hi * 4 + y_lo), z: 8, core: 2. Of those that a mesh axis runs over, the one named last changes fastest.
Arguments:
- orbitals: float32 [256, 4, 384, 256], P('orb', None, 'grid'), may hold values from -6 to 6
- potential: float32 [4, 384, 256], P(None, 'grid'), may hold values from -1.5 to 0
- rotation: bfloat16 [256, 256], replicated, may hold values from -0.375 to 0.375
Outputs:
- rotated: float32 [256, 4, 384, 256], P('orb', None, 'grid')
The draws below stay inside these ranges and needn't reach their ends.
All inputs are finite; a program needn't handle non-finite values.
Results may differ from the reference program's by a relative error of at most 0.0029.
Values may be sent and summed in bfloat16 or wider, within the bound.
No kernel may reach another device: no remote copies, remote signals or barrier semaphores. Data moves between devices by JAX's collectives and lax.ppermute only.
A program may use at most 64 MiB of HBM per device.

```python
import jax
import jax.numpy as jnp
from jax import lax

NORB = 256
NY = 256
NZ = 4
NX = 384


def draw_orbitals(key, part):
    key = jax.random.fold_in(key, 11)
    return jnp.clip(jax.random.normal(key, (NORB, NZ, NX, NY), jnp.float32), -6.0, 6.0)


def levels(rng, shape, shards, low, high):
    gain, own = 1.0, jax.random.fold_in(rng, 6)
    for position, parts in shards:
        draws = jnp.exp(jax.random.uniform(jax.random.fold_in(own, position), (parts,), jnp.float32, low / len(shards), high / len(shards)))
        gain = gain * jnp.repeat(draws, shape[position] // parts).reshape([-1 if axis == position else 1 for axis in range(len(shape))])
    return gain


def scatter_about(key, extent, scale, most, kind=jnp.bfloat16):
    return jnp.clip(scale * jax.random.normal(key, extent, jnp.float32), -most, most).astype(kind)


def setup_inputs(seed: int = 0) -> dict:
    streams_of = jax.random.split(jax.random.key(seed), 4)
    orbitals = draw_orbitals(jax.random.fold_in(streams_of[3], 71), 0)
    potential = jnp.clip(-1.5 + 1.5 * jax.random.uniform(streams_of[1], (NZ, NX, NY), jnp.float32) ** levels(streams_of[1], (NZ, NX, NY), ((1, 16),), -0.2, 0.2), -1.5, 0.0)
    rotation = scatter_about(streams_of[2], (NORB, NORB), NORB ** -0.5, 0.375)
    return {"orbitals": orbitals, "potential": potential, "rotation": rotation}


STENCIL = (-5369.0 / 1800.0, 12.0 / 7.0, -15.0 / 56.0, 10.0 / 189.0, -1.0 / 112.0, 2.0 / 1925.0, -1.0 / 16632.0)
centre_value = 9.0
spread_value = 7.0


def hamiltonian(values, potential):
    layers = values.shape[1]
    height = values.shape[2]
    breadth = values.shape[3]
    side_x = jnp.pad(values, ((0, 0), (0, 0), (6, 6), (0, 0)))
    side_y = jnp.pad(values, ((0, 0), (0, 0), (0, 0), (6, 6)))
    side_z = jnp.pad(values, ((0, 0), (6, 6), (0, 0), (0, 0)))
    summed = (3.0 * STENCIL[0]) * values
    for offset in range(1, 7):
        part_x = side_x[:, :, 6 + offset:6 + offset + height] + side_x[:, :, 6 - offset:6 - offset + height]
        part_y = side_y[:, :, :, 6 + offset:6 + offset + breadth] + side_y[:, :, :, 6 - offset:6 - offset + breadth]
        part_z = side_z[:, 6 + offset:6 + offset + layers] + side_z[:, 6 - offset:6 - offset + layers]
        summed = summed + STENCIL[offset] * (part_x + part_y + part_z)
    return -0.5 * summed + potential * values


def chebyshev(values, potential):
    previous = values
    current = (hamiltonian(values, potential) - centre_value * values) / spread_value
    for degree in range(2):
        following = 2.0 * (hamiltonian(current, potential) - centre_value * current) / spread_value - previous
        previous = current
        current = following
    return current


def reference(orbitals, potential, rotation):
    blocks = orbitals.reshape(NORB // 16, 16, NZ, NX, NY)
    filtered = lax.map(lambda block_values: chebyshev(block_values, potential).astype(jnp.bfloat16), blocks)
    flattened = filtered.reshape(NORB, NZ * NX * NY)
    rotated = jnp.dot(rotation.T, flattened, preferred_element_type=jnp.float32)
    return rotated.reshape(NORB, NZ, NX, NY)
```

```python
import jax
import jax.numpy as jnp
import numpy as np
from jax import lax
from jax.experimental import pallas as pl
from jax.experimental.pallas import tpu as pltpu
from jax.sharding import PartitionSpec as P

STENCIL = (
    -5369.0 / 1800.0,
    12.0 / 7.0,
    -15.0 / 56.0,
    10.0 / 189.0,
    -1.0 / 112.0,
    2.0 / 1925.0,
    -1.0 / 16632.0,
)
CENTRE = 9.0
SPREAD = 7.0
REACH = 6
TAPS = tuple(-0.5 * s / SPREAD for s in STENCIL)
DIAGONAL = (-CENTRE - 1.5 * STENCIL[0]) / SPREAD
VMEM_LIMIT = 40 * 1024 * 1024
WHOLE = pl.BlockSpec(memory_space=pltpu.VMEM)


def band_matrix(breadth):
    band = np.zeros((breadth, breadth), np.float64)
    for offset in range(1, REACH + 1):
        band += TAPS[offset] * (np.eye(breadth, k=offset) + np.eye(breadth, k=-offset))
    high = band.astype(jnp.bfloat16)
    low = (band - high.astype(np.float64)).astype(jnp.bfloat16)
    return np.stack([high, low])


def call(kernel, out_shape, *args, scratch=(), flops=0, **kwargs):
    moved = sum(a.size * a.dtype.itemsize for a in args)
    return pl.pallas_call(
        kernel,
        out_shape=out_shape,
        in_specs=[WHOLE] * len(args),
        out_specs=jax.tree.map(lambda _: WHOLE, out_shape),
        scratch_shapes=list(scratch),
        compiler_params=pltpu.CompilerParams(vmem_limit_bytes=VMEM_LIMIT),
        cost_estimate=pl.CostEstimate(flops=flops, bytes_accessed=moved, transcendentals=0),
        **kwargs,
    )(*args)


def pack(orbitals, potential, count, layers, height):
    breadth = orbitals.shape[2]
    halo, near = 3 * REACH, 2 * REACH
    rows = layers * halo * count + layers * near

    def kernel(x_ref, p_ref, own_ref, head_ref, tail_ref):
        for layer in range(layers):
            own = jnp.concatenate(
                [
                    jnp.swapaxes(x_ref[:, layer * height + r : layer * height + r + 8, :], 0, 1)
                    for r in range(0, height, 8)
                ],
                axis=0,
            )
            own_ref[layer * height * count : (layer + 1) * height * count, :] = own.reshape(-1, breadth)
            here = slice(layer * halo * count, (layer + 1) * halo * count)
            head_ref[here, :] = own[:halo].reshape(-1, breadth).astype(jnp.bfloat16)
            tail_ref[here, :] = own[height - halo :].reshape(-1, breadth).astype(jnp.bfloat16)
        for out_ref, first in ((head_ref, 0), (tail_ref, height - near)):
            strips = [
                p_ref[layer * height + first : layer * height + first + near, :] for layer in range(layers)
            ]
            out_ref[layers * halo * count :, :] = jnp.concatenate(strips, axis=0).astype(jnp.bfloat16)

    shape = jax.ShapeDtypeStruct((rows, breadth), jnp.bfloat16)
    own = jax.ShapeDtypeStruct((layers * height * count, breadth), jnp.float32)
    return call(kernel, (own, shape, shape), orbitals, potential)


def filtering(own, potential, before, after, inside, count, layers, height):
    breadth = own.shape[1]
    halo, near = 3 * REACH, 2 * REACH
    tall = (height + 2 * halo, height + 2 * near, height + 2 * REACH, height)

    def kernel(x_ref, p_ref, before_ref, after_ref, band_ref, inside_ref, out_ref, v0, d1, d2, w):
        for layer in range(layers):
            base = layer * tall[0] * count
            source = slice(layer * halo * count, (layer + 1) * halo * count)
            v0[base : base + halo * count, :] = before_ref[source, :].astype(jnp.float32)
            base += (halo + height) * count
            v0[base : base + halo * count, :] = after_ref[source, :].astype(jnp.float32)
            base -= height * count
            v0[base : base + height * count, :] = x_ref[
                layer * height * count : (layer + 1) * height * count, :
            ]
        strips = layers * halo * count
        for layer in range(layers):
            base = layer * tall[1]
            source = slice(strips + layer * near, strips + (layer + 1) * near)
            w[base : base + near, :] = before_ref[source, :].astype(jnp.float32) * (1.0 / SPREAD) + DIAGONAL
            w[base + near : base + near + height, :] = (
                p_ref[layer * height : (layer + 1) * height, :] * (1.0 / SPREAD) + DIAGONAL
            )
            base += near + height
            w[base : base + near, :] = after_ref[source, :].astype(jnp.float32) * (1.0 / SPREAD) + DIAGONAL

        high, low = band_ref[0], band_ref[1]

        def along_y(src, src_tall, layer, dst_tall):
            start = (layer * src_tall + REACH) * count
            u = src[start : start + dst_tall * count, :]
            u_high = u.astype(jnp.bfloat16)
            u_low = (u - u_high.astype(jnp.float32)).astype(jnp.bfloat16)

            def dot(a, b):
                return jnp.dot(a, b, preferred_element_type=jnp.float32)

            return dot(u_high, high) + (dot(u_low, high) + dot(u_high, low))

        def stage(number, src, dst, previous):
            src_tall, dst_tall = tall[number - 1], tall[number]
            outer = (dst_tall - height) // 2
            for layer in range(layers):
                dst[layer * dst_tall * count : (layer + 1) * dst_tall * count, :] = along_y(
                    src, src_tall, layer, dst_tall
                )
            blocks = dst_tall // REACH

            def step(b, carry):
                if outer:
                    keep = jnp.where(
                        b < outer // REACH,
                        inside_ref[0],
                        jnp.where(b >= blocks - outer // REACH, inside_ref[1], 1.0),
                    )
                centres = []
                for layer in range(layers):
                    first = (layer * src_tall + b * REACH + REACH) * count
                    first = pl.multiple_of(first, 8)
                    centres.append(src[pl.ds(first, REACH * count), :].reshape(REACH, count, breadth))
                for layer in range(layers):
                    first = pl.multiple_of((layer * src_tall + b * REACH) * count, 8)
                    u = src[pl.ds(first, 3 * REACH * count), :].reshape(3 * REACH, count, breadth)
                    place = pl.multiple_of((layer * dst_tall + b * REACH) * count, 8)
                    here = pl.ds(place, REACH * count)
                    total = dst[here, :].reshape(REACH, count, breadth)
                    w_first = layer * tall[1] + (near - outer) + b * REACH
                    diagonal = jnp.stack(
                        [
                            jnp.broadcast_to(w[pl.ds(w_first + r, 1), :], (count, breadth))
                            for r in range(REACH)
                        ]
                    )
                    total = total + diagonal * centres[layer]
                    for offset in range(1, REACH + 1):
                        pair = u[REACH - offset : 2 * REACH - offset] + u[REACH + offset : 2 * REACH + offset]
                        if offset < layers:
                            if layer - offset >= 0:
                                pair = pair + centres[layer - offset]
                            if layer + offset < layers:
                                pair = pair + centres[layer + offset]
                        total = total + TAPS[offset] * pair
                    if number > 1:
                        prev_tall = tall[number - 2]
                        p_first = (layer * prev_tall + b * REACH + 2 * REACH) * count
                        p_first = pl.multiple_of(p_first, 8)
                        before_last = previous[pl.ds(p_first, REACH * count), :].reshape(
                            REACH, count, breadth
                        )
                        total = 2.0 * total - before_last
                    if outer:
                        total = total * keep
                    total = total.reshape(REACH * count, breadth)
                    if number == 3:
                        out_ref[here, :] = total.astype(jnp.bfloat16)
                    else:
                        dst[here, :] = total
                return carry

            lax.fori_loop(0, blocks, step, 0)

        stage(1, v0, d1, None)
        stage(2, d1, d2, v0)
        stage(3, d2, v0, d1)

    scratch = [pltpu.VMEM((layers * t * count, breadth), jnp.float32) for t in tall[:3]]
    scratch.append(pltpu.VMEM((layers * tall[1], breadth), jnp.float32))
    band = jnp.asarray(band_matrix(breadth))
    return pl.pallas_call(
        kernel,
        out_shape=jax.ShapeDtypeStruct((layers * height * count, breadth), jnp.bfloat16),
        in_specs=[WHOLE] * 5 + [pl.BlockSpec(memory_space=pltpu.SMEM)],
        out_specs=WHOLE,
        scratch_shapes=scratch,
        compiler_params=pltpu.CompilerParams(vmem_limit_bytes=VMEM_LIMIT),
        cost_estimate=pl.CostEstimate(flops=2 * 3456 * 256 * 768, bytes_accessed=3 << 20, transcendentals=0),
    )(own, potential, before, after, band, inside)


def rotate(blocks, rotation, parts, per, count):
    rows, breadth = blocks.shape
    total = parts * count

    def kernel(g_ref, r_ref, out_ref):
        cells = g_ref[...].astype(jnp.float32).reshape(parts, per, count, breadth)
        turn = r_ref[...]
        outs = []
        for r in range(per):
            part = cells[:, r].reshape(total, breadth).astype(jnp.bfloat16)
            product = lax.dot_general(
                turn, part, (((0,), (0,)), ((), ())), preferred_element_type=jnp.float32
            )
            outs.append(product.reshape(parts, 1, count, breadth))
        result = jnp.concatenate(outs, axis=1).reshape(rows, breadth)
        out_ref[...] = result.astype(jnp.bfloat16)

    return call(
        kernel,
        jax.ShapeDtypeStruct((rows, breadth), jnp.bfloat16),
        blocks,
        rotation,
        flops=2 * total * rows * breadth,
    )


def unpack(rows, count, cells):
    breadth = rows.shape[1]

    def kernel(q_ref, out_ref):
        for first in range(0, cells, 8):
            group = q_ref[first * count : (first + 8) * count, :].astype(jnp.float32)
            out_ref[:, first : first + 8, :] = jnp.swapaxes(group.reshape(8, count, breadth), 0, 1)

    return call(kernel, jax.ShapeDtypeStruct((count, cells, breadth), jnp.float32), rows)


def local(orbitals, potential, rotation):
    count, layers, height, breadth = orbitals.shape
    cells = layers * height
    parts = lax.axis_size("orb")
    columns = lax.axis_size("grid")
    orbitals = orbitals.reshape(count, cells, breadth)
    potential = potential.reshape(cells, breadth)
    own, head, tail = pack(orbitals, potential, count, layers, height)
    before = lax.ppermute(tail, "grid", [(i, i + 1) for i in range(columns - 1)])
    after = lax.ppermute(head, "grid", [(i + 1, i) for i in range(columns - 1)])
    place = lax.axis_index("grid")
    inside = jnp.stack([place > 0, place < columns - 1]).astype(jnp.float32)
    filtered = filtering(own, potential, before, after, inside, count, layers, height)
    per = cells // parts
    filtered = filtered.reshape(parts, per * count, breadth)
    gathered = lax.all_to_all(filtered, "orb", 0, 0, tiled=True)
    rotated = rotate(gathered.reshape(cells * count, breadth), rotation, parts, per, count)
    returned = lax.all_to_all(rotated.reshape(parts, per * count, breadth), "orb", 0, 0, tiled=True)
    result = unpack(returned.reshape(cells * count, breadth), count, cells)
    return result.reshape(count, layers, height, breadth)


def solution(mesh):
    return jax.shard_map(
        local,
        mesh=mesh,
        in_specs=(P("orb", None, "grid", None), P(None, "grid", None), P()),
        out_specs=P("orb", None, "grid", None),
        check_vma=False,
    )
```

```python
import jax
import jax.numpy as jnp
import numpy as np
from jax import lax
from jax.experimental import pallas as pl
from jax.experimental.pallas import tpu as pltpu
from jax.sharding import PartitionSpec as P

STENCIL = (
    -5369.0 / 1800.0,
    12.0 / 7.0,
    -15.0 / 56.0,
    10.0 / 189.0,
    -1.0 / 112.0,
    2.0 / 1925.0,
    -1.0 / 16632.0,
)
CENTRE = 9.0
SPREAD = 7.0
REACH = 6
HALO = 3 * REACH
NEAR = 2 * REACH
TAPS = tuple(-0.5 * s / SPREAD for s in STENCIL)
DIAGONAL = (-CENTRE - 1.5 * STENCIL[0]) / SPREAD
RUN = 4
ROWS = 12
LANES = 128
VMEM_LIMIT = 40 * 1024 * 1024
PACK_LIMIT = 60 * 1024 * 1024
IN_VMEM = pl.BlockSpec(memory_space=pltpu.VMEM)
IN_HBM = pl.BlockSpec(memory_space=pltpu.HBM)


def band_matrices(breadth):
    band = np.zeros((breadth, breadth), np.float64)
    for offset in range(1, REACH + 1):
        band += TAPS[offset] * (np.eye(breadth, k=offset) + np.eye(breadth, k=-offset))
    head = band.astype(jnp.bfloat16)
    rest = (band - head.astype(np.float64)).astype(jnp.bfloat16)
    two = np.asarray(2, jnp.bfloat16)
    return np.stack([head, rest, head * two, rest * two])


def call(kernel, out_shape, in_specs, args, scratch=(), out_specs=None, flops=0, moved=1 << 20, limit=VMEM_LIMIT):
    return pl.pallas_call(
        kernel,
        out_shape=out_shape,
        in_specs=list(in_specs),
        out_specs=jax.tree.map(lambda _: IN_VMEM, out_shape) if out_specs is None else out_specs,
        scratch_shapes=list(scratch),
        compiler_params=pltpu.CompilerParams(vmem_limit_bytes=limit),
        cost_estimate=pl.CostEstimate(flops=flops, bytes_accessed=moved, transcendentals=0),
    )(*args)


def pack(orbitals, potential, layers, height):
    count, cells, breadth = orbitals.shape
    halo_rows = layers * HALO * count
    shape = (halo_rows + layers * NEAR, breadth)

    def kernel(x_hbm, p_hbm, *refs):
        outs, (x_ref, p_ref), held, (sems, out_sems) = refs[:3], refs[3:5], refs[5:8], refs[8:]
        ends = lax.rem(lax.axis_index("grid"), RUN) == RUN - 1
        fetches = [
            pltpu.make_async_copy(x_hbm.at[:, pl.ds(at * height, height), :], x_ref.at[at], sems.at[at])
            for at in range(layers)
        ] + [pltpu.make_async_copy(p_hbm, p_ref, sems.at[layers])]
        for fetch in fetches:
            fetch.start()
        sent = []

        def put(part, here, head, tail):
            for place, rows in enumerate((head, tail, jnp.where(ends, tail, head))):
                held[place][here, :] = rows
            for place in range(3):
                copy = pltpu.make_async_copy(
                    held[place].at[here, :], outs[place].at[here, :], out_sems.at[part, place]
                )
                copy.start()
                sent.append(copy)

        for layer in range(layers):
            fetches[layer].wait()
            own = jnp.concatenate(
                [jnp.swapaxes(x_ref[layer, :, r : r + 8, :], 0, 1) for r in range(0, height, 8)], axis=0
            )
            put(
                layer,
                slice(layer * HALO * count, (layer + 1) * HALO * count),
                own[:HALO].reshape(-1, breadth).astype(jnp.bfloat16),
                own[height - HALO :].reshape(-1, breadth).astype(jnp.bfloat16),
            )
        fetches[layers].wait()
        first, final = (
            jnp.concatenate(
                [p_ref[at * height + r : at * height + r + NEAR, :] for at in range(layers)], axis=0
            ).astype(jnp.bfloat16)
            for r in (0, height - NEAR)
        )
        put(layers, slice(halo_rows, shape[0]), first, final)
        for copy in sent:
            copy.wait()

    halo = jax.ShapeDtypeStruct(shape, jnp.bfloat16)
    return call(
        kernel,
        (halo, halo, halo),
        [IN_HBM] * 2,
        (orbitals, potential),
        scratch=[
            pltpu.VMEM((layers, count, height, breadth), jnp.float32),
            pltpu.VMEM((cells, breadth), jnp.float32),
        ]
        + [pltpu.VMEM(shape, jnp.bfloat16)] * 3
        + [pltpu.SemaphoreType.DMA((layers + 1,)), pltpu.SemaphoreType.DMA((layers + 1, 3))],
        out_specs=(IN_HBM,) * 3,
        limit=PACK_LIMIT,
    )


def dot(a, b):
    return jnp.dot(a, b, preferred_element_type=jnp.float32)


def along_y(u, head, rest):
    u_head = u.astype(jnp.bfloat16)
    u_rest = (u - u_head.astype(jnp.float32)).astype(jnp.bfloat16)
    if JOIN:
        return dot(
            jnp.concatenate([u_head, u_rest, u_head], axis=1), jnp.concatenate([head, head, rest], axis=0)
        )
    return dot(u_head, head) + (dot(u_rest, head) + dot(u_head, rest))


JOIN = True


class Block:
    def __init__(self, count, layers, height, breadth):
        self.count, self.layers, self.height, self.breadth = count, layers, height, breadth
        self.tall = (height + 2 * HALO, height + 2 * NEAR, height + 2 * REACH, height)

    def shape(self, stage):
        return (self.layers * self.tall[stage] * self.count, self.breadth)

    def diagonals(self):
        return (2, self.layers, self.tall[1], self.breadth)

    def at(self, stage, layer, first, size):
        start = (layer * self.tall[stage] + first) * self.count
        return slice(start, start + size * self.count)

    def set_diagonal(self, w, layer, first, potential):
        scaled = potential * (1.0 / SPREAD) + DIAGONAL
        w[0, layer, first : first + potential.shape[0], :] = scaled
        w[1, layer, first : first + potential.shape[0], :] = scaled * 2.0

    def step(self, number, first, size, src, y, w, previous, dst):
        outer = (self.tall[number] - self.height) // 2
        scale = 1.0 if number == 1 else 2.0
        for layer in range(self.layers):
            for lane in range(0, self.breadth, LANES):
                lanes = slice(lane, lane + LANES)

                def rows(ref, stage, at_layer, start, length):
                    return ref[self.at(stage, at_layer, start, length), lanes].reshape(length, self.count, LANES)

                u = rows(src, number - 1, layer, first, size + 2 * REACH)
                start = first + NEAR - outer
                diagonal = jnp.concatenate(
                    [
                        jnp.broadcast_to(w[int(number > 1), layer, start + r : start + r + 1, lanes], (1, self.count, LANES))
                        for r in range(size)
                    ],
                    axis=0,
                )
                total = rows(y, number, layer, first, size) + diagonal * u[REACH : REACH + size]
                for offset in range(1, REACH + 1):
                    low, high = REACH - offset, REACH + offset
                    pair = u[low : low + size] + u[high : high + size]
                    for other in (layer - offset, layer + offset):
                        if 0 <= other < self.layers:
                            pair = pair + rows(src, number - 1, other, first + REACH, size)
                    total = total + (scale * TAPS[offset]) * pair
                if number > 1:
                    total = total - rows(previous, number - 2, layer, first + 2 * REACH, size)
                dst[self.at(number, layer, first, size), lanes] = total.reshape(-1, LANES).astype(dst.dtype)

    def follow(self, number, first, size, src, y, band):
        which = 0 if number == 1 else 2
        for layer in range(self.layers):
            u = src[self.at(number - 1, layer, first + REACH, size), :]
            y[self.at(number, layer, first, size), :] = along_y(u, band[which], band[which + 1])


def prepare(orbitals, potential, band, block):
    height = block.height
    inner = height - 2 * REACH

    def kernel(x_ref, p_ref, band_ref, v0, y1, d1, y2, w):
        for layer in range(block.layers):
            for r in range(0, height, 8):
                first = layer * height + r
                rows = jnp.swapaxes(x_ref[:, first : first + 8, :], 0, 1)
                v0[block.at(0, layer, HALO + r, 8), :] = rows.reshape(-1, block.breadth)
            block.set_diagonal(w, layer, NEAR, p_ref[layer * height : (layer + 1) * height, :])
        block.follow(1, NEAR, height, v0, y1, band_ref)
        block.step(1, NEAR + REACH, inner, v0, y1, w, None, d1)
        block.follow(2, NEAR, inner, d1, y2, band_ref)

    return call(
        kernel,
        tuple(
            jax.ShapeDtypeStruct(s, jnp.float32)
            for s in (block.shape(0), block.shape(1), block.shape(1), block.shape(2), block.diagonals())
        ),
        [IN_VMEM] * 3,
        (orbitals, potential, band),
        flops=6 * 768 * 256 * 256,
        moved=4 << 20,
    )


def filtering(prepared, before, after, wrap, band, block):
    layers, height, count, breadth = block.layers, block.height, block.count, block.breadth
    strips = layers * HALO * count

    def kernel(v0_in, y1_in, d1_in, y2_in, w_in, before_ref, after_ref, wrap_ref, band_ref, out_ref, v0, y1, d1, y2, w, d2, y3):
        place = lax.axis_index("grid")
        in_run = lax.rem(place, RUN)
        opens = (in_run == 0).astype(jnp.float32)
        closes = (in_run == RUN - 1).astype(jnp.float32)

        def sides(source):
            wrapped = wrap_ref[source, :].astype(jnp.float32)
            left = before_ref[source, :].astype(jnp.float32) + opens * wrapped
            return left, after_ref[source, :].astype(jnp.float32) + closes * wrapped

        for layer in range(layers):
            left, right = sides(slice(layer * HALO * count, (layer + 1) * HALO * count))
            v0[block.at(0, layer, 0, HALO), :] = left
            v0[block.at(0, layer, HALO + height, HALO), :] = right
            left, right = sides(slice(strips + layer * NEAR, strips + (layer + 1) * NEAR))
            block.set_diagonal(w, layer, 0, left)
            block.set_diagonal(w, layer, NEAR + height, right)

        def outside(number, ref, at_stage, rows):
            tall = block.tall[at_stage]

            @pl.when(place == 0)
            def _():
                for layer in range(layers):
                    here = block.at(at_stage, layer, 0, rows)
                    ref[here, :] = jnp.zeros((rows * count, breadth), jnp.float32)

            @pl.when(place == lax.axis_size("grid") - 1)
            def _():
                for layer in range(layers):
                    here = block.at(at_stage, layer, tall - rows, rows)
                    ref[here, :] = jnp.zeros((rows * count, breadth), jnp.float32)

        tall = block.tall
        block.follow(1, 0, NEAR, v0, y1, band_ref)
        block.follow(1, NEAR + height, NEAR, v0, y1, band_ref)
        low, high = NEAR + REACH, NEAR + height - REACH
        block.step(1, NEAR, REACH, v0, y1, w, None, d1)
        block.follow(2, REACH, REACH, d1, y2, band_ref)
        block.step(1, high, REACH, v0, y1, w, None, d1)
        block.follow(2, high - REACH, REACH, d1, y2, band_ref)
        block.step(1, 0, NEAR, v0, y1, w, None, d1)
        block.follow(2, 0, REACH, d1, y2, band_ref)
        block.step(1, NEAR + height, NEAR, v0, y1, w, None, d1)
        block.follow(2, REACH + height, REACH, d1, y2, band_ref)
        outside(1, d1, 1, NEAR)
        outside(1, y2, 2, REACH)
        for first in range(0, tall[2], ROWS):
            block.step(2, first, ROWS, d1, y2, w, v0, d2)
            start, stop = max(first, REACH), min(first + ROWS, REACH + height)
            block.follow(3, start - REACH, stop - start, d2, y3, band_ref)
        outside(2, d2, 2, REACH)
        for first in range(0, height, ROWS):
            block.step(3, first, ROWS, d2, y3, w, d1, out_ref)

    f32 = jnp.float32
    out_shape = (jax.ShapeDtypeStruct(block.shape(3), jnp.bfloat16),) + tuple(
        jax.ShapeDtypeStruct(a.shape, f32) for a in prepared
    )
    return pl.pallas_call(
        kernel,
        out_shape=out_shape,
        in_specs=[IN_VMEM] * 9,
        out_specs=(IN_VMEM,) * 6,
        scratch_shapes=[pltpu.VMEM(block.shape(2), f32), pltpu.VMEM(block.shape(3), f32)],
        input_output_aliases={i: i + 1 for i in range(5)},
        compiler_params=pltpu.CompilerParams(vmem_limit_bytes=VMEM_LIMIT),
        cost_estimate=pl.CostEstimate(flops=2 * 3456 * 256 * 768, bytes_accessed=3 << 20, transcendentals=0),
    )(*prepared, before, after, wrap, band)[0]


def rotate(blocks, rotation, parts, per, count):
    rows, breadth = blocks.shape
    total = parts * count

    def kernel(g_ref, r_ref, out_ref):
        cells = g_ref[...].astype(jnp.float32).reshape(parts, per, count, breadth)
        turn = r_ref[...]
        outs = []
        for r in range(per):
            part = cells[:, r].reshape(total, breadth).astype(jnp.bfloat16)
            product = lax.dot_general(
                turn, part, (((0,), (0,)), ((), ())), preferred_element_type=jnp.float32
            )
            outs.append(product.reshape(parts, 1, count, breadth))
        result = jnp.concatenate(outs, axis=1).reshape(rows, breadth)
        out_ref[...] = result.astype(jnp.bfloat16)

    return call(
        kernel,
        jax.ShapeDtypeStruct((rows, breadth), jnp.bfloat16),
        [IN_VMEM, IN_VMEM],
        (blocks, rotation),
        flops=2 * total * rows * breadth,
    )


def unpack(rows, count, layers, height):
    breadth = rows.shape[1]

    def kernel(q_ref, out_hbm, held, sems):
        copies = []
        for layer in range(layers):
            for r in range(0, height, 8):
                first = layer * height + r
                group = q_ref[first * count : (first + 8) * count, :].astype(jnp.float32)
                held[layer, :, r : r + 8, :] = jnp.swapaxes(group.reshape(8, count, breadth), 0, 1)
            copy = pltpu.make_async_copy(
                held.at[layer], out_hbm.at[:, pl.ds(layer * height, height), :], sems.at[layer]
            )
            copy.start()
            copies.append(copy)
        for copy in copies:
            copy.wait()

    return call(
        kernel,
        jax.ShapeDtypeStruct((count, layers * height, breadth), jnp.float32),
        [IN_VMEM],
        (rows,),
        scratch=[
            pltpu.VMEM((layers, count, height, breadth), jnp.float32),
            pltpu.SemaphoreType.DMA((layers,)),
        ],
        out_specs=IN_HBM,
    )


def local(orbitals, potential, rotation):
    count, layers, height, breadth = orbitals.shape
    cells = layers * height
    parts = lax.axis_size("orb")
    columns = lax.axis_size("grid")
    block = Block(count, layers, height, breadth)
    band = jnp.asarray(band_matrices(breadth))
    orbitals = orbitals.reshape(count, cells, breadth)
    potential = potential.reshape(cells, breadth)
    head, tail, wrapped = pack(orbitals, potential, layers, height)
    inner = [i for i in range(columns - 1) if i % RUN != RUN - 1]
    outer = [i for i in range(columns - 1) if i % RUN == RUN - 1]
    before = lax.ppermute(tail, "grid", [(i, i + 1) for i in inner])
    after = lax.ppermute(head, "grid", [(i + 1, i) for i in inner])
    wrap = lax.ppermute(wrapped, "grid", [(i, i + 1) for i in outer] + [(i + 1, i) for i in outer])
    prepared = prepare(orbitals, potential, band, block)
    filtered = filtering(prepared, before, after, wrap, band, block)
    per = cells // parts
    filtered = filtered.reshape(parts, per * count, breadth)
    gathered = lax.all_to_all(filtered, "orb", 0, 0, tiled=True)
    rotated = rotate(gathered.reshape(cells * count, breadth), rotation, parts, per, count)
    returned = lax.all_to_all(rotated.reshape(parts, per * count, breadth), "orb", 0, 0, tiled=True)
    result = unpack(returned.reshape(cells * count, breadth), count, layers, height)
    return result.reshape(count, layers, height, breadth)


def solution(mesh):
    return jax.shard_map(
        local,
        mesh=mesh,
        in_specs=(P("orb", None, "grid", None), P(None, "grid", None), P()),
        out_specs=P("orb", None, "grid", None),
        check_vma=False,
    )
```

```python
import jax
import jax.numpy as jnp
import numpy as np
from jax import lax
from jax.experimental import pallas as pl
from jax.experimental.pallas import tpu as pltpu
from jax.sharding import PartitionSpec as P

STENCIL = (
    -5369.0 / 1800.0,
    12.0 / 7.0,
    -15.0 / 56.0,
    10.0 / 189.0,
    -1.0 / 112.0,
    2.0 / 1925.0,
    -1.0 / 16632.0,
)
CENTRE = 9.0
SPREAD = 7.0
REACH = 6
HALO = 3 * REACH
NEAR = 2 * REACH
TAPS = tuple(-0.5 * s / SPREAD for s in STENCIL)
DIAGONAL = (-CENTRE - 1.5 * STENCIL[0]) / SPREAD
RUN = 4
ROWS = 12
LANES = 128
VMEM_LIMIT = 40 * 1024 * 1024
IN_VMEM = pl.BlockSpec(memory_space=pltpu.VMEM)
IN_HBM = pl.BlockSpec(memory_space=pltpu.HBM)


def band_matrices(breadth):
    band = np.zeros((breadth, breadth), np.float64)
    for offset in range(1, REACH + 1):
        band += TAPS[offset] * (np.eye(breadth, k=offset) + np.eye(breadth, k=-offset))
    head = band.astype(jnp.bfloat16)
    rest = (band - head.astype(np.float64)).astype(jnp.bfloat16)
    two = np.asarray(2, jnp.bfloat16)
    return np.stack([head, rest, head * two, rest * two])


def call(kernel, out_shape, in_specs, args, scratch=(), out_specs=None, flops=0, moved=1 << 20):
    return pl.pallas_call(
        kernel,
        out_shape=out_shape,
        in_specs=list(in_specs),
        out_specs=jax.tree.map(lambda _: IN_VMEM, out_shape) if out_specs is None else out_specs,
        scratch_shapes=list(scratch),
        compiler_params=pltpu.CompilerParams(vmem_limit_bytes=VMEM_LIMIT),
        cost_estimate=pl.CostEstimate(flops=flops, bytes_accessed=moved, transcendentals=0),
    )(*args)


def pack(orbitals, potential, layers, height):
    count, cells, breadth = orbitals.shape
    halo_rows = layers * HALO * count
    shape = (halo_rows + layers * NEAR, breadth)

    def kernel(x_hbm, p_hbm, head_ref, tail_ref, wrap_ref, x_ref, p_ref, sems):
        ends = lax.rem(lax.axis_index("grid"), RUN) == RUN - 1
        fetches = [
            pltpu.make_async_copy(x_hbm.at[:, pl.ds(at * height, height), :], x_ref.at[at], sems.at[at])
            for at in range(layers)
        ] + [pltpu.make_async_copy(p_hbm, p_ref, sems.at[layers])]
        for fetch in fetches:
            fetch.start()

        def put(here, head, tail):
            head_ref[here, :] = head
            tail_ref[here, :] = tail
            wrap_ref[here, :] = jnp.where(ends, tail, head)

        for layer in range(layers):
            fetches[layer].wait()
            own = jnp.concatenate(
                [jnp.swapaxes(x_ref[layer, :, r : r + 8, :], 0, 1) for r in range(0, height, 8)], axis=0
            )
            put(
                slice(layer * HALO * count, (layer + 1) * HALO * count),
                own[:HALO].reshape(-1, breadth).astype(jnp.bfloat16),
                own[height - HALO :].reshape(-1, breadth).astype(jnp.bfloat16),
            )
        fetches[layers].wait()
        first, final = (
            jnp.concatenate(
                [p_ref[at * height + r : at * height + r + NEAR, :] for at in range(layers)], axis=0
            ).astype(jnp.bfloat16)
            for r in (0, height - NEAR)
        )
        put(slice(halo_rows, shape[0]), first, final)

    halo = jax.ShapeDtypeStruct(shape, jnp.bfloat16)
    return call(
        kernel,
        (halo, halo, halo),
        [IN_HBM] * 2,
        [pltpu.with_memory_space_constraint(a, pltpu.HBM) for a in (orbitals, potential)],
        scratch=[
            pltpu.VMEM((layers, count, height, breadth), jnp.float32),
            pltpu.VMEM((cells, breadth), jnp.float32),
            pltpu.SemaphoreType.DMA((layers + 1,)),
        ],
    )


def dot(a, b):
    return jnp.dot(a, b, preferred_element_type=jnp.float32)


def along_y(u, head, rest, exact):
    u_head = u.astype(jnp.bfloat16)
    if exact:
        return dot(jnp.concatenate([u_head, u_head], axis=1), jnp.concatenate([head, rest], axis=0))
    u_rest = (u - u_head.astype(jnp.float32)).astype(jnp.bfloat16)
    return dot(jnp.concatenate([u_head, u_rest, u_head], axis=1), jnp.concatenate([head, head, rest], axis=0))


class Block:
    def __init__(self, count, layers, height, breadth):
        self.count, self.layers, self.height, self.breadth = count, layers, height, breadth
        self.tall = (height + 2 * HALO, height + 2 * NEAR, height + 2 * REACH, height)

    def shape(self, stage):
        return (self.layers * self.tall[stage] * self.count, self.breadth)

    def diagonals(self):
        return (2, self.layers, self.tall[1], self.breadth)

    def at(self, stage, layer, first, size):
        start = (layer * self.tall[stage] + first) * self.count
        return slice(start, start + size * self.count)

    def set_diagonal(self, w, layer, first, potential):
        scaled = potential * (1.0 / SPREAD) + DIAGONAL
        w[0, layer, first : first + potential.shape[0], :] = scaled
        w[1, layer, first : first + potential.shape[0], :] = scaled * 2.0

    def step(self, number, first, size, src, y, w, previous, dst, keep=None):
        outer = (self.tall[number] - self.height) // 2
        scale = 1.0 if number == 1 else 2.0
        for layer in range(self.layers):
            for lane in range(0, self.breadth, LANES):
                lanes = slice(lane, lane + LANES)

                def rows(ref, stage, at_layer, start, length):
                    return ref[self.at(stage, at_layer, start, length), lanes].reshape(length, self.count, LANES)

                u = rows(src, number - 1, layer, first, size + 2 * REACH)
                start = first + NEAR - outer
                diagonal = jnp.concatenate(
                    [
                        jnp.broadcast_to(w[int(number > 1), layer, start + r : start + r + 1, lanes], (1, self.count, LANES))
                        for r in range(size)
                    ],
                    axis=0,
                )
                total = rows(y, number, layer, first, size) + diagonal * u[REACH : REACH + size]
                for offset in range(1, REACH + 1):
                    low, high = REACH - offset, REACH + offset
                    pair = u[low : low + size] + u[high : high + size]
                    for other in (layer - offset, layer + offset):
                        if 0 <= other < self.layers:
                            pair = pair + rows(src, number - 1, other, first + REACH, size)
                    total = total + (scale * TAPS[offset]) * pair
                if number > 1:
                    total = total - rows(previous, number - 2, layer, first + 2 * REACH, size)
                if keep is not None:
                    some, scalar = keep
                    total = jnp.concatenate(
                        [total[:some] * scalar, total[some:]] if some > 0 else [total[:some], total[some:] * scalar], axis=0
                    ) if abs(some) < size else total * scalar
                dst[self.at(number, layer, first, size), lanes] = total.reshape(-1, LANES).astype(dst.dtype)

    def follow(self, number, firsts, size, src, y, band, exact=False):
        which = 0 if number == 1 else 2
        places = [(layer, first) for first in firsts for layer in range(self.layers)]
        u = [src[self.at(number - 1, layer, first + REACH, size), :] for layer, first in places]
        result = along_y(jnp.concatenate(u, axis=0), band[which], band[which + 1], exact)
        for i, (layer, first) in enumerate(places):
            y[self.at(number, layer, first, size), :] = result[i * size * self.count : (i + 1) * size * self.count]


def prepare(orbitals, potential, band, block):
    height = block.height
    inner = height - 2 * REACH

    def kernel(x_ref, p_ref, band_ref, v0, y1, d1, y2, w):
        for layer in range(block.layers):
            for r in range(0, height, 8):
                first = layer * height + r
                rows = jnp.swapaxes(x_ref[:, first : first + 8, :], 0, 1)
                v0[block.at(0, layer, HALO + r, 8), :] = rows.reshape(-1, block.breadth)
            block.set_diagonal(w, layer, NEAR, p_ref[layer * height : (layer + 1) * height, :])
        block.follow(1, [NEAR], height, v0, y1, band_ref)
        block.step(1, NEAR + REACH, inner, v0, y1, w, None, d1)
        block.follow(2, [NEAR], inner, d1, y2, band_ref)

    return call(
        kernel,
        tuple(
            jax.ShapeDtypeStruct(s, jnp.float32)
            for s in (block.shape(0), block.shape(1), block.shape(1), block.shape(2), block.diagonals())
        ),
        [IN_VMEM] * 3,
        (orbitals, potential, band),
        flops=6 * 768 * 256 * 256,
        moved=4 << 20,
    )


def filtering(prepared, before, after, wrap, band, block):
    layers, height, count, breadth = block.layers, block.height, block.count, block.breadth
    strips = layers * HALO * count

    def kernel(v0_in, y1_in, d1_in, y2_in, w_in, before_ref, after_ref, wrap_ref, band_ref, out_ref, v0, y1, d1, y2, w, d2, y3):
        place = lax.axis_index("grid")
        in_run = lax.rem(place, RUN)
        opens = (in_run == 0).astype(jnp.float32)
        closes = (in_run == RUN - 1).astype(jnp.float32)

        def sides(source):
            wrapped = wrap_ref[source, :].astype(jnp.float32)
            left = before_ref[source, :].astype(jnp.float32) + opens * wrapped
            return left, after_ref[source, :].astype(jnp.float32) + closes * wrapped

        for layer in range(layers):
            left, right = sides(slice(layer * HALO * count, (layer + 1) * HALO * count))
            v0[block.at(0, layer, 0, HALO), :] = left
            v0[block.at(0, layer, HALO + height, HALO), :] = right
            left, right = sides(slice(strips + layer * NEAR, strips + (layer + 1) * NEAR))
            block.set_diagonal(w, layer, 0, left)
            block.set_diagonal(w, layer, NEAR + height, right)

        left = (place > 0).astype(jnp.float32)
        right = (place < lax.axis_size("grid") - 1).astype(jnp.float32)
        tall = block.tall
        low, high = NEAR + REACH, NEAR + height - REACH
        block.follow(1, [0, NEAR + height], NEAR, v0, y1, band_ref, exact=True)
        for first in (NEAR, high):
            block.step(1, first, REACH, v0, y1, w, None, d1)
            block.follow(2, [first - REACH], REACH, d1, y2, band_ref)
        block.step(1, 0, NEAR, v0, y1, w, None, d1, (NEAR, left))
        block.follow(2, [0], REACH, d1, y2, band_ref)
        block.step(1, NEAR + height, NEAR, v0, y1, w, None, d1, (NEAR, right))
        block.follow(2, [REACH + height], REACH, d1, y2, band_ref)
        for first in range(0, tall[2], ROWS):
            keep = {0: (REACH, left), tall[2] - ROWS: (-REACH, right)}.get(first)
            block.step(2, first, ROWS, d1, y2, w, v0, d2, keep)
            start, stop = max(first, REACH), min(first + ROWS, REACH + height)
            block.follow(3, [start - REACH], stop - start, d2, y3, band_ref)
        for first in range(0, height, ROWS):
            block.step(3, first, ROWS, d2, y3, w, d1, out_ref)

    f32 = jnp.float32
    out_shape = (jax.ShapeDtypeStruct(block.shape(3), jnp.bfloat16),) + tuple(
        jax.ShapeDtypeStruct(a.shape, f32) for a in prepared
    )
    return pl.pallas_call(
        kernel,
        out_shape=out_shape,
        in_specs=[IN_VMEM] * 9,
        out_specs=(IN_VMEM,) * 6,
        scratch_shapes=[pltpu.VMEM(block.shape(2), f32), pltpu.VMEM(block.shape(3), f32)],
        input_output_aliases={i: i + 1 for i in range(5)},
        compiler_params=pltpu.CompilerParams(vmem_limit_bytes=VMEM_LIMIT),
        cost_estimate=pl.CostEstimate(flops=2 * 3456 * 256 * 768, bytes_accessed=3 << 20, transcendentals=0),
    )(*prepared, before, after, wrap, band)[0]


def rotate(blocks, rotation, parts, per, count):
    rows, breadth = blocks.shape
    total = parts * count

    def kernel(g_ref, r_ref, out_ref):
        cells = g_ref[...].astype(jnp.float32).reshape(parts, per, count, breadth)
        turn = r_ref[...]
        outs = []
        for r in range(per):
            part = cells[:, r].reshape(total, breadth).astype(jnp.bfloat16)
            product = lax.dot_general(
                turn, part, (((0,), (0,)), ((), ())), preferred_element_type=jnp.float32
            )
            outs.append(product.reshape(parts, 1, count, breadth))
        result = jnp.concatenate(outs, axis=1).reshape(rows, breadth)
        out_ref[...] = result.astype(jnp.bfloat16)

    return call(
        kernel,
        jax.ShapeDtypeStruct((rows, breadth), jnp.bfloat16),
        [IN_VMEM, IN_VMEM],
        (blocks, rotation),
        flops=2 * total * rows * breadth,
    )


def unpack(rows, count, layers, height):
    breadth = rows.shape[1]

    def kernel(q_ref, out_hbm, held, sems):
        copies = []
        for layer in range(layers):
            for r in range(0, height, 8):
                first = layer * height + r
                group = q_ref[first * count : (first + 8) * count, :].astype(jnp.float32)
                held[layer, :, r : r + 8, :] = jnp.swapaxes(group.reshape(8, count, breadth), 0, 1)
            copy = pltpu.make_async_copy(
                held.at[layer], out_hbm.at[:, pl.ds(layer * height, height), :], sems.at[layer]
            )
            copy.start()
            copies.append(copy)
        for copy in copies:
            copy.wait()

    return call(
        kernel,
        jax.ShapeDtypeStruct((count, layers * height, breadth), jnp.float32),
        [IN_VMEM],
        (rows,),
        scratch=[
            pltpu.VMEM((layers, count, height, breadth), jnp.float32),
            pltpu.SemaphoreType.DMA((layers,)),
        ],
        out_specs=IN_HBM,
    )


def local(orbitals, potential, rotation):
    count, layers, height, breadth = orbitals.shape
    cells = layers * height
    parts = lax.axis_size("orb")
    columns = lax.axis_size("grid")
    block = Block(count, layers, height, breadth)
    band = jnp.asarray(band_matrices(breadth))
    orbitals = orbitals.reshape(count, cells, breadth)
    potential = potential.reshape(cells, breadth)
    head, tail, wrapped = pack(orbitals, potential, layers, height)
    inner = [i for i in range(columns - 1) if i % RUN != RUN - 1]
    outer = [i for i in range(columns - 1) if i % RUN == RUN - 1]
    before = lax.ppermute(tail, "grid", [(i, i + 1) for i in inner])
    after = lax.ppermute(head, "grid", [(i + 1, i) for i in inner])
    wrap = lax.ppermute(wrapped, "grid", [(i, i + 1) for i in outer] + [(i + 1, i) for i in outer])
    prepared = prepare(orbitals, potential, band, block)
    filtered = filtering(prepared, before, after, wrap, band, block)
    per = cells // parts
    filtered = filtered.reshape(parts, per * count, breadth)
    gathered = lax.all_to_all(filtered, "orb", 0, 0, tiled=True)
    rotated = rotate(gathered.reshape(cells * count, breadth), rotation, parts, per, count)
    returned = lax.all_to_all(rotated.reshape(parts, per * count, breadth), "orb", 0, 0, tiled=True)
    result = unpack(returned.reshape(cells * count, breadth), count, layers, height)
    return result.reshape(count, layers, height, breadth)


def solution(mesh):
    return jax.shard_map(
        local,
        mesh=mesh,
        in_specs=(P("orb", None, "grid", None), P(None, "grid", None), P()),
        out_specs=P("orb", None, "grid", None),
        check_vma=False,
    )
```

```python
import jax
import jax.numpy as jnp
import numpy as np
from jax import lax
from jax.experimental import pallas as pl
from jax.experimental.pallas import tpu as pltpu
from jax.sharding import PartitionSpec as P

STENCIL = (
    -5369.0 / 1800.0,
    12.0 / 7.0,
    -15.0 / 56.0,
    10.0 / 189.0,
    -1.0 / 112.0,
    2.0 / 1925.0,
    -1.0 / 16632.0,
)
CENTRE = 9.0
SPREAD = 7.0
REACH = 6
HALO = 3 * REACH
NEAR = 2 * REACH
TAPS = tuple(-0.5 * s / SPREAD for s in STENCIL)
DIAGONAL = (-CENTRE - 1.5 * STENCIL[0]) / SPREAD
RUN = 4
ROWS = 12
LANES = 128
VMEM_LIMIT = 40 * 1024 * 1024
IN_VMEM = pl.BlockSpec(memory_space=pltpu.VMEM)
IN_HBM = pl.BlockSpec(memory_space=pltpu.HBM)


def band_matrices(breadth):
    band = np.zeros((breadth, breadth), np.float64)
    for offset in range(1, REACH + 1):
        band += TAPS[offset] * (np.eye(breadth, k=offset) + np.eye(breadth, k=-offset))
    head = band.astype(jnp.bfloat16)
    rest = (band - head.astype(np.float64)).astype(jnp.bfloat16)
    two = np.asarray(2, jnp.bfloat16)
    return np.stack([head, rest, head * two, rest * two])


def call(kernel, out_shape, in_specs, args, scratch=(), out_specs=None, flops=0, moved=1 << 20):
    return pl.pallas_call(
        kernel,
        out_shape=out_shape,
        in_specs=list(in_specs),
        out_specs=jax.tree.map(lambda _: IN_VMEM, out_shape) if out_specs is None else out_specs,
        scratch_shapes=list(scratch),
        compiler_params=pltpu.CompilerParams(vmem_limit_bytes=VMEM_LIMIT),
        cost_estimate=pl.CostEstimate(flops=flops, bytes_accessed=moved, transcendentals=0),
    )(*args)


def pack(orbitals, potential, layers, height):
    count, cells, breadth = orbitals.shape
    halo_rows = layers * HALO * count
    shape = (halo_rows + layers * NEAR, breadth)

    def kernel(x_hbm, p_hbm, head_ref, tail_ref, wrap_ref, x_ref, p_ref, sems):
        ends = lax.rem(lax.axis_index("grid"), RUN) == RUN - 1
        fetches = [
            pltpu.make_async_copy(x_hbm.at[:, pl.ds(at * height, height), :], x_ref.at[at], sems.at[at])
            for at in range(layers)
        ] + [pltpu.make_async_copy(p_hbm, p_ref, sems.at[layers])]
        for fetch in fetches:
            fetch.start()

        def put(here, head, tail):
            head_ref[here, :] = head
            tail_ref[here, :] = tail
            wrap_ref[here, :] = jnp.where(ends, tail, head)

        for layer in range(layers):
            fetches[layer].wait()
            own = jnp.concatenate(
                [jnp.swapaxes(x_ref[layer, :, r : r + 8, :], 0, 1) for r in range(0, height, 8)], axis=0
            )
            put(
                slice(layer * HALO * count, (layer + 1) * HALO * count),
                own[:HALO].reshape(-1, breadth).astype(jnp.bfloat16),
                own[height - HALO :].reshape(-1, breadth).astype(jnp.bfloat16),
            )
        fetches[layers].wait()
        first, final = (
            jnp.concatenate(
                [p_ref[at * height + r : at * height + r + NEAR, :] for at in range(layers)], axis=0
            ).astype(jnp.bfloat16)
            for r in (0, height - NEAR)
        )
        put(slice(halo_rows, shape[0]), first, final)

    halo = jax.ShapeDtypeStruct(shape, jnp.bfloat16)
    return call(
        kernel,
        (halo, halo, halo),
        [IN_HBM] * 2,
        [pltpu.with_memory_space_constraint(a, pltpu.HBM) for a in (orbitals, potential)],
        scratch=[
            pltpu.VMEM((layers, count, height, breadth), jnp.float32),
            pltpu.VMEM((cells, breadth), jnp.float32),
            pltpu.SemaphoreType.DMA((layers + 1,)),
        ],
    )


def dot(a, b):
    return jnp.dot(a, b, preferred_element_type=jnp.float32)


def along_y(u, head, rest, exact):
    u_head = u.astype(jnp.bfloat16)
    if exact:
        return dot(jnp.concatenate([u_head, u_head], axis=1), jnp.concatenate([head, rest], axis=0))
    u_rest = (u - u_head.astype(jnp.float32)).astype(jnp.bfloat16)
    return dot(jnp.concatenate([u_head, u_rest, u_head], axis=1), jnp.concatenate([head, head, rest], axis=0))


class Block:
    def __init__(self, count, layers, height, breadth):
        self.count, self.layers, self.height, self.breadth = count, layers, height, breadth
        self.tall = (height + 2 * HALO, height + 2 * NEAR, height + 2 * REACH, height)

    def shape(self, stage):
        return (self.layers * self.tall[stage] * self.count, self.breadth)

    def diagonals(self):
        return (2, self.layers, self.tall[1], self.breadth)

    def at(self, stage, layer, first, size):
        start = (layer * self.tall[stage] + first) * self.count
        return slice(start, start + size * self.count)

    def set_diagonal(self, w, layer, first, potential):
        scaled = potential * (1.0 / SPREAD) + DIAGONAL
        w[0, layer, first : first + potential.shape[0], :] = scaled
        w[1, layer, first : first + potential.shape[0], :] = scaled * 2.0

    def step(self, number, first, size, src, y, w, previous, dst, keep=None):
        outer = (self.tall[number] - self.height) // 2
        scale = 1.0 if number == 1 else 2.0
        for layer in range(self.layers):
            for lane in range(0, self.breadth, LANES):
                lanes = slice(lane, lane + LANES)

                def rows(ref, stage, at_layer, start, length):
                    return ref[self.at(stage, at_layer, start, length), lanes].reshape(length, self.count, LANES)

                u = rows(src, number - 1, layer, first, size + 2 * REACH)
                start = first + NEAR - outer
                diagonal = jnp.concatenate(
                    [
                        jnp.broadcast_to(w[int(number > 1), layer, start + r : start + r + 1, lanes], (1, self.count, LANES))
                        for r in range(size)
                    ],
                    axis=0,
                )
                total = rows(y, number, layer, first, size) + diagonal * u[REACH : REACH + size]
                for offset in range(1, REACH + 1):
                    low, high = REACH - offset, REACH + offset
                    pair = u[low : low + size] + u[high : high + size]
                    for other in (layer - offset, layer + offset):
                        if 0 <= other < self.layers:
                            pair = pair + rows(src, number - 1, other, first + REACH, size)
                    total = total + (scale * TAPS[offset]) * pair
                if number > 1:
                    total = total - rows(previous, number - 2, layer, first + 2 * REACH, size)
                if keep is not None:
                    some, scalar = keep
                    total = jnp.concatenate(
                        [total[:some] * scalar, total[some:]] if some > 0 else [total[:some], total[some:] * scalar], axis=0
                    ) if abs(some) < size else total * scalar
                dst[self.at(number, layer, first, size), lanes] = total.reshape(-1, LANES).astype(dst.dtype)

    def follow(self, number, firsts, size, src, y, band, exact=False):
        which = 0 if number == 1 else 2
        places = [(layer, first) for first in firsts for layer in range(self.layers)]
        u = [src[self.at(number - 1, layer, first + REACH, size), :] for layer, first in places]
        result = along_y(jnp.concatenate(u, axis=0), band[which], band[which + 1], exact)
        for i, (layer, first) in enumerate(places):
            y[self.at(number, layer, first, size), :] = result[i * size * self.count : (i + 1) * size * self.count]


def prepare(orbitals, potential, band, block):
    height = block.height
    inner = height - 2 * REACH

    def kernel(x_ref, p_ref, band_ref, v0, y1, d1, y2, w):
        for layer in range(block.layers):
            for r in range(0, height, 8):
                first = layer * height + r
                rows = jnp.swapaxes(x_ref[:, first : first + 8, :], 0, 1)
                v0[block.at(0, layer, HALO + r, 8), :] = rows.reshape(-1, block.breadth)
            block.set_diagonal(w, layer, NEAR, p_ref[layer * height : (layer + 1) * height, :])
        block.follow(1, [NEAR], height, v0, y1, band_ref)
        block.step(1, NEAR + REACH, inner, v0, y1, w, None, d1)
        block.follow(2, [NEAR], inner, d1, y2, band_ref)

    return call(
        kernel,
        tuple(
            jax.ShapeDtypeStruct(s, jnp.float32)
            for s in (block.shape(0), block.shape(1), block.shape(1), block.shape(2), block.diagonals())
        ),
        [IN_VMEM] * 3,
        (orbitals, potential, band),
        flops=6 * 768 * 256 * 256,
        moved=4 << 20,
    )


def filtering(prepared, before, after, wrap, band, block):
    layers, height, count, breadth = block.layers, block.height, block.count, block.breadth
    strips = layers * HALO * count

    def kernel(v0_in, y1_in, d1_in, y2_in, w_in, before_ref, after_ref, wrap_ref, band_ref, out_ref, v0, y1, d1, y2, w, d2, y3):
        place = lax.axis_index("grid")
        in_run = lax.rem(place, RUN)
        opens = (in_run == 0).astype(jnp.float32)
        closes = (in_run == RUN - 1).astype(jnp.float32)

        def sides(source):
            wrapped = wrap_ref[source, :].astype(jnp.float32)
            left = before_ref[source, :].astype(jnp.float32) + opens * wrapped
            return left, after_ref[source, :].astype(jnp.float32) + closes * wrapped

        for layer in range(layers):
            left, right = sides(slice(layer * HALO * count, (layer + 1) * HALO * count))
            v0[block.at(0, layer, 0, HALO), :] = left
            v0[block.at(0, layer, HALO + height, HALO), :] = right
            left, right = sides(slice(strips + layer * NEAR, strips + (layer + 1) * NEAR))
            block.set_diagonal(w, layer, 0, left)
            block.set_diagonal(w, layer, NEAR + height, right)

        left = (place > 0).astype(jnp.float32)
        right = (place < lax.axis_size("grid") - 1).astype(jnp.float32)
        tall = block.tall
        low, high = NEAR + REACH, NEAR + height - REACH
        block.follow(1, [0, NEAR + height], NEAR, v0, y1, band_ref, exact=True)
        block.step(1, NEAR, REACH, v0, y1, w, None, d1)
        block.step(1, high, REACH, v0, y1, w, None, d1)
        block.follow(2, [low - 2 * REACH, high - REACH], REACH, d1, y2, band_ref)
        block.step(1, 0, NEAR, v0, y1, w, None, d1, (NEAR, left))
        block.step(1, NEAR + height, NEAR, v0, y1, w, None, d1, (NEAR, right))
        block.follow(2, [0, REACH + height], REACH, d1, y2, band_ref)
        block.step(2, NEAR, height - NEAR, d1, y2, w, v0, d2)
        block.follow(3, [REACH], height - NEAR, d2, y3, band_ref)
        block.step(2, 0, NEAR, d1, y2, w, v0, d2, (REACH, left))
        block.step(2, height, NEAR, d1, y2, w, v0, d2, (-REACH, right))
        block.follow(3, [0, height - REACH], REACH, d2, y3, band_ref)
        block.step(3, REACH, height - NEAR, d2, y3, w, d1, out_ref)
        block.step(3, 0, REACH, d2, y3, w, d1, out_ref)
        block.step(3, height - REACH, REACH, d2, y3, w, d1, out_ref)

    f32 = jnp.float32
    out_shape = (jax.ShapeDtypeStruct(block.shape(3), jnp.bfloat16),) + tuple(
        jax.ShapeDtypeStruct(a.shape, f32) for a in prepared
    )
    return pl.pallas_call(
        kernel,
        out_shape=out_shape,
        in_specs=[IN_VMEM] * 9,
        out_specs=(IN_VMEM,) * 6,
        scratch_shapes=[pltpu.VMEM(block.shape(2), f32), pltpu.VMEM(block.shape(3), f32)],
        input_output_aliases={i: i + 1 for i in range(5)},
        compiler_params=pltpu.CompilerParams(vmem_limit_bytes=VMEM_LIMIT),
        cost_estimate=pl.CostEstimate(flops=2 * 3456 * 256 * 768, bytes_accessed=3 << 20, transcendentals=0),
    )(*prepared, before, after, wrap, band)[0]


def rotate(blocks, rotation, parts, per, count):
    rows, breadth = blocks.shape
    total = parts * count

    def kernel(g_ref, r_ref, out_ref):
        cells = g_ref[...].astype(jnp.float32).reshape(parts, per, count, breadth)
        turn = r_ref[...]
        outs = []
        for r in range(per):
            part = cells[:, r].reshape(total, breadth).astype(jnp.bfloat16)
            product = lax.dot_general(
                turn, part, (((0,), (0,)), ((), ())), preferred_element_type=jnp.float32
            )
            outs.append(product.reshape(parts, 1, count, breadth))
        result = jnp.concatenate(outs, axis=1).reshape(rows, breadth)
        out_ref[...] = result.astype(jnp.bfloat16)

    return call(
        kernel,
        jax.ShapeDtypeStruct((rows, breadth), jnp.bfloat16),
        [IN_VMEM, IN_VMEM],
        (blocks, rotation),
        flops=2 * total * rows * breadth,
    )


def unpack(rows, count, layers, height):
    breadth = rows.shape[1]

    def kernel(q_ref, out_hbm, held, sems):
        copies = []
        for layer in range(layers):
            for r in range(0, height, 8):
                first = layer * height + r
                group = q_ref[first * count : (first + 8) * count, :].astype(jnp.float32)
                held[layer, :, r : r + 8, :] = jnp.swapaxes(group.reshape(8, count, breadth), 0, 1)
            copy = pltpu.make_async_copy(
                held.at[layer], out_hbm.at[:, pl.ds(layer * height, height), :], sems.at[layer]
            )
            copy.start()
            copies.append(copy)
        for copy in copies:
            copy.wait()

    return call(
        kernel,
        jax.ShapeDtypeStruct((count, layers * height, breadth), jnp.float32),
        [IN_VMEM],
        (rows,),
        scratch=[
            pltpu.VMEM((layers, count, height, breadth), jnp.float32),
            pltpu.SemaphoreType.DMA((layers,)),
        ],
        out_specs=IN_HBM,
    )


def local(orbitals, potential, rotation):
    count, layers, height, breadth = orbitals.shape
    cells = layers * height
    parts = lax.axis_size("orb")
    columns = lax.axis_size("grid")
    block = Block(count, layers, height, breadth)
    band = jnp.asarray(band_matrices(breadth))
    orbitals = orbitals.reshape(count, cells, breadth)
    potential = potential.reshape(cells, breadth)
    head, tail, wrapped = pack(orbitals, potential, layers, height)
    inner = [i for i in range(columns - 1) if i % RUN != RUN - 1]
    outer = [i for i in range(columns - 1) if i % RUN == RUN - 1]
    before = lax.ppermute(tail, "grid", [(i, i + 1) for i in inner])
    after = lax.ppermute(head, "grid", [(i + 1, i) for i in inner])
    wrap = lax.ppermute(wrapped, "grid", [(i, i + 1) for i in outer] + [(i + 1, i) for i in outer])
    prepared = prepare(orbitals, potential, band, block)
    filtered = filtering(prepared, before, after, wrap, band, block)
    per = cells // parts
    filtered = filtered.reshape(parts, per * count, breadth)
    gathered = lax.all_to_all(filtered, "orb", 0, 0, tiled=True)
    rotated = rotate(gathered.reshape(cells * count, breadth), rotation, parts, per, count)
    returned = lax.all_to_all(rotated.reshape(parts, per * count, breadth), "orb", 0, 0, tiled=True)
    result = unpack(returned.reshape(cells * count, breadth), count, layers, height)
    return result.reshape(count, layers, height, breadth)


def solution(mesh):
    return jax.shard_map(
        local,
        mesh=mesh,
        in_specs=(P("orb", None, "grid", None), P(None, "grid", None), P()),
        out_specs=P("orb", None, "grid", None),
        check_vma=False,
    )
```

```python
import jax
import jax.numpy as jnp
import numpy as np
from jax import lax
from jax.experimental import pallas as pl
from jax.experimental.pallas import tpu as pltpu
from jax.sharding import PartitionSpec as P

STENCIL = (
    -5369.0 / 1800.0,
    12.0 / 7.0,
    -15.0 / 56.0,
    10.0 / 189.0,
    -1.0 / 112.0,
    2.0 / 1925.0,
    -1.0 / 16632.0,
)
CENTRE = 9.0
SPREAD = 7.0
REACH = 6
HALO = 3 * REACH
NEAR = 2 * REACH
TAPS = tuple(-0.5 * s / SPREAD for s in STENCIL)
DIAGONAL = (-CENTRE - 1.5 * STENCIL[0]) / SPREAD
RUN = 4
ROWS = 12
LANES = 128
VMEM_LIMIT = 40 * 1024 * 1024
IN_VMEM = pl.BlockSpec(memory_space=pltpu.VMEM)
IN_HBM = pl.BlockSpec(memory_space=pltpu.HBM)


def band_matrices(breadth):
    band = np.zeros((breadth, breadth), np.float64)
    for offset in range(1, REACH + 1):
        band += TAPS[offset] * (np.eye(breadth, k=offset) + np.eye(breadth, k=-offset))
    head = band.astype(jnp.bfloat16)
    rest = (band - head.astype(np.float64)).astype(jnp.bfloat16)
    two = np.asarray(2, jnp.bfloat16)
    return np.stack([head, rest, head * two, rest * two])


def call(kernel, out_shape, in_specs, args, scratch=(), out_specs=None, flops=0, moved=1 << 20):
    return pl.pallas_call(
        kernel,
        out_shape=out_shape,
        in_specs=list(in_specs),
        out_specs=jax.tree.map(lambda _: IN_VMEM, out_shape) if out_specs is None else out_specs,
        scratch_shapes=list(scratch),
        compiler_params=pltpu.CompilerParams(vmem_limit_bytes=VMEM_LIMIT),
        cost_estimate=pl.CostEstimate(flops=flops, bytes_accessed=moved, transcendentals=0),
    )(*args)


def pack(orbitals, potential, layers, height):
    count, cells, breadth = orbitals.shape
    halo_rows = layers * HALO * count
    shape = (halo_rows + layers * NEAR, breadth)

    def kernel(x_hbm, p_hbm, head_ref, tail_ref, wrap_ref, x_ref, p_ref, sems):
        ends = lax.rem(lax.axis_index("grid"), RUN) == RUN - 1
        fetches = [
            pltpu.make_async_copy(x_hbm.at[:, pl.ds(at * height, height), :], x_ref.at[at], sems.at[at])
            for at in range(layers)
        ] + [pltpu.make_async_copy(p_hbm, p_ref, sems.at[layers])]
        for fetch in fetches:
            fetch.start()

        def put(here, head, tail):
            head_ref[here, :] = head
            tail_ref[here, :] = tail
            wrap_ref[here, :] = jnp.where(ends, tail, head)

        for layer in range(layers):
            fetches[layer].wait()
            own = jnp.concatenate(
                [jnp.swapaxes(x_ref[layer, :, r : r + 8, :], 0, 1) for r in range(0, height, 8)], axis=0
            )
            put(
                slice(layer * HALO * count, (layer + 1) * HALO * count),
                own[:HALO].reshape(-1, breadth).astype(jnp.bfloat16),
                own[height - HALO :].reshape(-1, breadth).astype(jnp.bfloat16),
            )
        fetches[layers].wait()
        first, final = (
            jnp.concatenate(
                [p_ref[at * height + r : at * height + r + NEAR, :] for at in range(layers)], axis=0
            ).astype(jnp.bfloat16)
            for r in (0, height - NEAR)
        )
        put(slice(halo_rows, shape[0]), first, final)

    halo = jax.ShapeDtypeStruct(shape, jnp.bfloat16)
    return call(
        kernel,
        (halo, halo, halo),
        [IN_HBM] * 2,
        [pltpu.with_memory_space_constraint(a, pltpu.HBM) for a in (orbitals, potential)],
        scratch=[
            pltpu.VMEM((layers, count, height, breadth), jnp.float32),
            pltpu.VMEM((cells, breadth), jnp.float32),
            pltpu.SemaphoreType.DMA((layers + 1,)),
        ],
    )


def dot(a, b):
    return jnp.dot(a, b, preferred_element_type=jnp.float32)


def along_y(u, head, rest, exact):
    u_head = u.astype(jnp.bfloat16)
    if exact:
        return dot(jnp.concatenate([u_head, u_head], axis=1), jnp.concatenate([head, rest], axis=0))
    u_rest = (u - u_head.astype(jnp.float32)).astype(jnp.bfloat16)
    return dot(jnp.concatenate([u_head, u_rest, u_head], axis=1), jnp.concatenate([head, head, rest], axis=0))


class Block:
    def __init__(self, count, layers, height, breadth):
        self.count, self.layers, self.height, self.breadth = count, layers, height, breadth
        self.tall = (height + 2 * HALO, height + 2 * NEAR, height + 2 * REACH, height)

    def shape(self, stage):
        return (self.layers * self.tall[stage] * self.count, self.breadth)

    def diagonals(self):
        return (2, self.layers, self.tall[1], self.breadth)

    def at(self, stage, layer, first, size):
        start = (layer * self.tall[stage] + first) * self.count
        return slice(start, start + size * self.count)

    def set_diagonal(self, w, layer, first, potential):
        scaled = potential * (1.0 / SPREAD) + DIAGONAL
        w[0, layer, first : first + potential.shape[0], :] = scaled
        w[1, layer, first : first + potential.shape[0], :] = scaled * 2.0

    def step(self, number, first, size, src, y, w, previous, dst, keep=None):
        outer = (self.tall[number] - self.height) // 2
        scale = 1.0 if number == 1 else 2.0
        for layer in range(self.layers):
            for lane in range(0, self.breadth, LANES):
                lanes = slice(lane, lane + LANES)

                def rows(ref, stage, at_layer, start, length):
                    return ref[self.at(stage, at_layer, start, length), lanes].reshape(length, self.count, LANES)

                u = rows(src, number - 1, layer, first, size + 2 * REACH)
                start = first + NEAR - outer
                diagonal = jnp.concatenate(
                    [
                        jnp.broadcast_to(w[int(number > 1), layer, start + r : start + r + 1, lanes], (1, self.count, LANES))
                        for r in range(size)
                    ],
                    axis=0,
                )
                total = rows(y, number, layer, first, size) + diagonal * u[REACH : REACH + size]
                for offset in range(1, REACH + 1):
                    low, high = REACH - offset, REACH + offset
                    pair = u[low : low + size] + u[high : high + size]
                    for other in (layer - offset, layer + offset):
                        if 0 <= other < self.layers:
                            pair = pair + rows(src, number - 1, other, first + REACH, size)
                    total = total + (scale * TAPS[offset]) * pair
                if number > 1:
                    total = total - rows(previous, number - 2, layer, first + 2 * REACH, size)
                if keep is not None:
                    some, scalar = keep
                    total = jnp.concatenate(
                        [total[:some] * scalar, total[some:]] if some > 0 else [total[:some], total[some:] * scalar], axis=0
                    ) if abs(some) < size else total * scalar
                dst[self.at(number, layer, first, size), lanes] = total.reshape(-1, LANES).astype(dst.dtype)

    def follow(self, number, firsts, size, src, y, band, exact=False):
        which = 0 if number == 1 else 2
        places = [(layer, first) for first in firsts for layer in range(self.layers)]
        u = [src[self.at(number - 1, layer, first + REACH, size), :] for layer, first in places]
        result = along_y(jnp.concatenate(u, axis=0), band[which], band[which + 1], exact)
        for i, (layer, first) in enumerate(places):
            y[self.at(number, layer, first, size), :] = result[i * size * self.count : (i + 1) * size * self.count]


def prepare(orbitals, potential, band, block):
    height = block.height
    inner = height - 2 * REACH

    def kernel(x_ref, p_ref, band_ref, v0, y1, d1, y2, w):
        for layer in range(block.layers):
            for r in range(0, height, 8):
                first = layer * height + r
                rows = jnp.swapaxes(x_ref[:, first : first + 8, :], 0, 1)
                v0[block.at(0, layer, HALO + r, 8), :] = rows.reshape(-1, block.breadth)
            block.set_diagonal(w, layer, NEAR, p_ref[layer * height : (layer + 1) * height, :])
        block.follow(1, [NEAR], height, v0, y1, band_ref)
        block.step(1, NEAR + REACH, inner, v0, y1, w, None, d1)
        block.follow(2, [NEAR], inner, d1, y2, band_ref)

    return call(
        kernel,
        tuple(
            jax.ShapeDtypeStruct(s, jnp.float32)
            for s in (block.shape(0), block.shape(1), block.shape(1), block.shape(2), block.diagonals())
        ),
        [IN_VMEM] * 3,
        (orbitals, potential, band),
        flops=6 * 768 * 256 * 256,
        moved=4 << 20,
    )


def left_side(block, halo, arrays, band, keep):
    v0, y1, d1, y2, w, d2, y3, out = arrays
    take_halo(block, halo, v0, w, 0)
    block.follow(1, [0], NEAR, v0, y1, band, exact=True)
    block.step(1, NEAR, REACH, v0, y1, w, None, d1)
    block.step(1, 0, NEAR, v0, y1, w, None, d1, (NEAR, keep))
    block.follow(2, [0], NEAR, d1, y2, band)
    block.step(2, NEAR, REACH, d1, y2, w, v0, d2)
    block.step(2, 0, NEAR, d1, y2, w, v0, d2, (REACH, keep))
    block.follow(3, [0], NEAR, d2, y3, band)
    block.step(3, 0, REACH, d2, y3, w, d1, out)


def right_side(block, halo, arrays, band, keep):
    v0, y1, d1, y2, w, d2, y3, out = arrays
    height = block.height
    take_halo(block, halo, v0, w, height)
    block.follow(1, [NEAR + height], NEAR, v0, y1, band, exact=True)
    block.step(1, NEAR + height - REACH, REACH, v0, y1, w, None, d1)
    block.step(1, NEAR + height, NEAR, v0, y1, w, None, d1, (NEAR, keep))
    block.follow(2, [height], NEAR, d1, y2, band)
    block.step(2, height - REACH, REACH, d1, y2, w, v0, d2)
    block.step(2, height, NEAR, d1, y2, w, v0, d2, (-REACH, keep))
    block.follow(3, [height - NEAR], NEAR, d2, y3, band)
    block.step(3, height - REACH, REACH, d2, y3, w, d1, out)


def take_halo(block, halo, v0, w, passed):
    count, layers = block.count, block.layers
    past = HALO if passed else 0
    for layer in range(layers):
        source = slice(layer * HALO * count, (layer + 1) * HALO * count)
        v0[block.at(0, layer, past + passed, HALO), :] = halo[source, :].astype(jnp.float32)
        source = slice(layers * HALO * count + layer * NEAR, layers * HALO * count + (layer + 1) * NEAR)
        block.set_diagonal(w, layer, passed + (NEAR if passed else 0), halo[source, :].astype(jnp.float32))


def filter_call(kernel, block, arrays, extra):
    given = [a for a in arrays if not isinstance(a, jax.ShapeDtypeStruct)]
    return pl.pallas_call(
        kernel,
        out_shape=tuple(jax.ShapeDtypeStruct(a.shape, a.dtype) for a in arrays),
        in_specs=[IN_VMEM] * (len(given) + len(extra)),
        out_specs=(IN_VMEM,) * len(arrays),
        input_output_aliases={i: i for i in range(len(given))},
        compiler_params=pltpu.CompilerParams(vmem_limit_bytes=VMEM_LIMIT),
        cost_estimate=pl.CostEstimate(flops=3456 * 256 * 768, bytes_accessed=3 << 20, transcendentals=0),
    )(*given, *extra)


def filtering(prepared, before, after, wrap, band, block):
    def place():
        at = lax.axis_index("grid")
        left = (at > 0).astype(jnp.float32)
        right = (at < lax.axis_size("grid") - 1).astype(jnp.float32)
        return lax.rem(at, RUN) == 0, lax.rem(at, RUN) == RUN - 1, left, right

    def early(*refs):
        before_ref, after_ref, band_ref = refs[5:8]
        arrays = refs[8:]
        opens, closes, left, right = place()

        @pl.when(jnp.logical_not(opens))
        def _():
            left_side(block, before_ref, arrays, band_ref, left)

        @pl.when(jnp.logical_not(closes))
        def _():
            right_side(block, after_ref, arrays, band_ref, right)

    def late(*refs):
        wrap_ref, band_ref = refs[8:10]
        arrays = refs[10:]
        v0, y1, d1, y2, w, d2, y3, out = arrays
        opens, closes, left, right = place()

        @pl.when(opens)
        def _():
            left_side(block, wrap_ref, arrays, band_ref, left)

        @pl.when(closes)
        def _():
            right_side(block, wrap_ref, arrays, band_ref, right)

        block.step(3, REACH, block.height - 2 * REACH, d2, y3, w, d1, out)

    made = (
        jax.ShapeDtypeStruct(block.shape(2), jnp.float32),
        jax.ShapeDtypeStruct(block.shape(3), jnp.float32),
        jax.ShapeDtypeStruct(block.shape(3), jnp.bfloat16),
    )
    arrays = filter_call(early, block, tuple(prepared) + made, (before, after, band))
    return filter_call(late, block, arrays, (wrap, band))[-1]


def rotate(blocks, rotation, parts, per, count):
    rows, breadth = blocks.shape
    total = parts * count

    def kernel(g_ref, r_ref, out_ref):
        cells = g_ref[...].astype(jnp.float32).reshape(parts, per, count, breadth)
        turn = r_ref[...]
        outs = []
        for r in range(per):
            part = cells[:, r].reshape(total, breadth).astype(jnp.bfloat16)
            product = lax.dot_general(
                turn, part, (((0,), (0,)), ((), ())), preferred_element_type=jnp.float32
            )
            outs.append(product.reshape(parts, 1, count, breadth))
        result = jnp.concatenate(outs, axis=1).reshape(rows, breadth)
        out_ref[...] = result.astype(jnp.bfloat16)

    return call(
        kernel,
        jax.ShapeDtypeStruct((rows, breadth), jnp.bfloat16),
        [IN_VMEM, IN_VMEM],
        (blocks, rotation),
        flops=2 * total * rows * breadth,
    )


def unpack(rows, count, layers, height):
    breadth = rows.shape[1]

    def kernel(q_ref, out_hbm, held, sems):
        copies = []
        for layer in range(layers):
            for r in range(0, height, 8):
                first = layer * height + r
                group = q_ref[first * count : (first + 8) * count, :].astype(jnp.float32)
                held[layer, :, r : r + 8, :] = jnp.swapaxes(group.reshape(8, count, breadth), 0, 1)
            copy = pltpu.make_async_copy(
                held.at[layer], out_hbm.at[:, pl.ds(layer * height, height), :], sems.at[layer]
            )
            copy.start()
            copies.append(copy)
        for copy in copies:
            copy.wait()

    return call(
        kernel,
        jax.ShapeDtypeStruct((count, layers * height, breadth), jnp.float32),
        [IN_VMEM],
        (rows,),
        scratch=[
            pltpu.VMEM((layers, count, height, breadth), jnp.float32),
            pltpu.SemaphoreType.DMA((layers,)),
        ],
        out_specs=IN_HBM,
    )


def local(orbitals, potential, rotation):
    count, layers, height, breadth = orbitals.shape
    cells = layers * height
    parts = lax.axis_size("orb")
    columns = lax.axis_size("grid")
    block = Block(count, layers, height, breadth)
    band = jnp.asarray(band_matrices(breadth))
    orbitals = orbitals.reshape(count, cells, breadth)
    potential = potential.reshape(cells, breadth)
    head, tail, wrapped = pack(orbitals, potential, layers, height)
    inner = [i for i in range(columns - 1) if i % RUN != RUN - 1]
    outer = [i for i in range(columns - 1) if i % RUN == RUN - 1]
    before = lax.ppermute(tail, "grid", [(i, i + 1) for i in inner])
    after = lax.ppermute(head, "grid", [(i + 1, i) for i in inner])
    wrap = lax.ppermute(wrapped, "grid", [(i, i + 1) for i in outer] + [(i + 1, i) for i in outer])
    prepared = prepare(orbitals, potential, band, block)
    filtered = filtering(prepared, before, after, wrap, band, block)
    per = cells // parts
    filtered = filtered.reshape(parts, per * count, breadth)
    gathered = lax.all_to_all(filtered, "orb", 0, 0, tiled=True)
    rotated = rotate(gathered.reshape(cells * count, breadth), rotation, parts, per, count)
    returned = lax.all_to_all(rotated.reshape(parts, per * count, breadth), "orb", 0, 0, tiled=True)
    result = unpack(returned.reshape(cells * count, breadth), count, layers, height)
    return result.reshape(count, layers, height, breadth)


def solution(mesh):
    return jax.shard_map(
        local,
        mesh=mesh,
        in_specs=(P("orb", None, "grid", None), P(None, "grid", None), P()),
        out_specs=P("orb", None, "grid", None),
        check_vma=False,
    )
```

```python
import jax
import jax.numpy as jnp
import numpy as np
from jax import lax
from jax.experimental import pallas as pl
from jax.experimental.pallas import tpu as pltpu
from jax.sharding import PartitionSpec as P

STENCIL = (
    -5369.0 / 1800.0,
    12.0 / 7.0,
    -15.0 / 56.0,
    10.0 / 189.0,
    -1.0 / 112.0,
    2.0 / 1925.0,
    -1.0 / 16632.0,
)
CENTRE = 9.0
SPREAD = 7.0
REACH = 6
HALO = 3 * REACH
NEAR = 2 * REACH
TAPS = tuple(-0.5 * s / SPREAD for s in STENCIL)
DIAGONAL = (-CENTRE - 1.5 * STENCIL[0]) / SPREAD
RUN = 4
ROWS = 12
LANES = 128
VMEM_LIMIT = 40 * 1024 * 1024
IN_VMEM = pl.BlockSpec(memory_space=pltpu.VMEM)
IN_HBM = pl.BlockSpec(memory_space=pltpu.HBM)


def band_matrices(breadth):
    band = np.zeros((breadth, breadth), np.float64)
    for offset in range(1, REACH + 1):
        band += TAPS[offset] * (np.eye(breadth, k=offset) + np.eye(breadth, k=-offset))
    head = band.astype(jnp.bfloat16)
    rest = (band - head.astype(np.float64)).astype(jnp.bfloat16)
    two = np.asarray(2, jnp.bfloat16)
    return np.stack([head, rest, head * two, rest * two])


def call(kernel, out_shape, in_specs, args, scratch=(), out_specs=None, flops=0, moved=1 << 20):
    return pl.pallas_call(
        kernel,
        out_shape=out_shape,
        in_specs=list(in_specs),
        out_specs=jax.tree.map(lambda _: IN_VMEM, out_shape) if out_specs is None else out_specs,
        scratch_shapes=list(scratch),
        compiler_params=pltpu.CompilerParams(vmem_limit_bytes=VMEM_LIMIT),
        cost_estimate=pl.CostEstimate(flops=flops, bytes_accessed=moved, transcendentals=0),
    )(*args)


def pack(orbitals, potential, layers, height):
    count, cells, breadth = orbitals.shape
    halo_rows = layers * HALO * count
    shape = (halo_rows + layers * NEAR, breadth)

    def kernel(x_hbm, p_hbm, head_ref, tail_ref, wrap_ref, x_ref, p_ref, sems):
        ends = lax.rem(lax.axis_index("grid"), RUN) == RUN - 1
        fetches = [
            pltpu.make_async_copy(x_hbm.at[:, pl.ds(at * height, height), :], x_ref.at[at], sems.at[at])
            for at in range(layers)
        ] + [pltpu.make_async_copy(p_hbm, p_ref, sems.at[layers])]
        for fetch in fetches:
            fetch.start()

        def put(here, head, tail):
            head_ref[here, :] = head
            tail_ref[here, :] = tail
            wrap_ref[here, :] = jnp.where(ends, tail, head)

        for layer in range(layers):
            fetches[layer].wait()
            own = jnp.concatenate(
                [jnp.swapaxes(x_ref[layer, :, r : r + 8, :], 0, 1) for r in range(0, height, 8)], axis=0
            )
            put(
                slice(layer * HALO * count, (layer + 1) * HALO * count),
                own[:HALO].reshape(-1, breadth).astype(jnp.bfloat16),
                own[height - HALO :].reshape(-1, breadth).astype(jnp.bfloat16),
            )
        fetches[layers].wait()
        first, final = (
            jnp.concatenate(
                [p_ref[at * height + r : at * height + r + NEAR, :] for at in range(layers)], axis=0
            ).astype(jnp.bfloat16)
            for r in (0, height - NEAR)
        )
        put(slice(halo_rows, shape[0]), first, final)

    halo = jax.ShapeDtypeStruct(shape, jnp.bfloat16)
    return call(
        kernel,
        (halo, halo, halo),
        [IN_HBM] * 2,
        [pltpu.with_memory_space_constraint(a, pltpu.HBM) for a in (orbitals, potential)],
        scratch=[
            pltpu.VMEM((layers, count, height, breadth), jnp.float32),
            pltpu.VMEM((cells, breadth), jnp.float32),
            pltpu.SemaphoreType.DMA((layers + 1,)),
        ],
    )


def dot(a, b):
    return jnp.dot(a, b, preferred_element_type=jnp.float32)


def along_y(u, head, rest, exact):
    u_head = u.astype(jnp.bfloat16)
    if exact:
        return dot(jnp.concatenate([u_head, u_head], axis=1), jnp.concatenate([head, rest], axis=0))
    u_rest = (u - u_head.astype(jnp.float32)).astype(jnp.bfloat16)
    return dot(jnp.concatenate([u_head, u_rest, u_head], axis=1), jnp.concatenate([head, head, rest], axis=0))


class Block:
    def __init__(self, count, layers, height, breadth):
        self.count, self.layers, self.height, self.breadth = count, layers, height, breadth
        self.tall = (height + 2 * HALO, height + 2 * NEAR, height + 2 * REACH, height)

    def shape(self, stage):
        return (self.layers * self.tall[stage] * self.count, self.breadth)

    def diagonals(self):
        return (2, self.layers, self.tall[1], self.breadth)

    def at(self, stage, layer, first, size):
        start = (layer * self.tall[stage] + first) * self.count
        return slice(start, start + size * self.count)

    def set_diagonal(self, w, layer, first, potential):
        scaled = potential * (1.0 / SPREAD) + DIAGONAL
        w[0, layer, first : first + potential.shape[0], :] = scaled
        w[1, layer, first : first + potential.shape[0], :] = scaled * 2.0

    def step(self, number, first, size, src, y, w, previous, dst, keep=None):
        outer = (self.tall[number] - self.height) // 2
        scale = 1.0 if number == 1 else 2.0
        for layer in range(self.layers):
            for lane in range(0, self.breadth, LANES):
                lanes = slice(lane, lane + LANES)

                def rows(ref, stage, at_layer, start, length):
                    return ref[self.at(stage, at_layer, start, length), lanes].reshape(length, self.count, LANES)

                u = rows(src, number - 1, layer, first, size + 2 * REACH)
                start = first + NEAR - outer
                diagonal = jnp.concatenate(
                    [
                        jnp.broadcast_to(w[int(number > 1), layer, start + r : start + r + 1, lanes], (1, self.count, LANES))
                        for r in range(size)
                    ],
                    axis=0,
                )
                total = rows(y, number, layer, first, size) + diagonal * u[REACH : REACH + size]
                for offset in range(1, REACH + 1):
                    low, high = REACH - offset, REACH + offset
                    pair = u[low : low + size] + u[high : high + size]
                    for other in (layer - offset, layer + offset):
                        if 0 <= other < self.layers:
                            pair = pair + rows(src, number - 1, other, first + REACH, size)
                    total = total + (scale * TAPS[offset]) * pair
                if number > 1:
                    total = total - rows(previous, number - 2, layer, first + 2 * REACH, size)
                if keep is not None:
                    some, scalar = keep
                    total = jnp.concatenate(
                        [total[:some] * scalar, total[some:]] if some > 0 else [total[:some], total[some:] * scalar], axis=0
                    ) if abs(some) < size else total * scalar
                dst[self.at(number, layer, first, size), lanes] = total.reshape(-1, LANES).astype(dst.dtype)

    def follow(self, number, firsts, size, src, y, band, exact=False):
        which = 0 if number == 1 else 2
        places = [(layer, first) for first in firsts for layer in range(self.layers)]
        u = [src[self.at(number - 1, layer, first + REACH, size), :] for layer, first in places]
        result = along_y(jnp.concatenate(u, axis=0), band[which], band[which + 1], exact)
        for i, (layer, first) in enumerate(places):
            y[self.at(number, layer, first, size), :] = result[i * size * self.count : (i + 1) * size * self.count]


def prepare(orbitals, potential, band, block):
    height = block.height
    inner = height - 2 * REACH

    def kernel(x_ref, p_ref, band_ref, v0, y1, d1, y2, w):
        for layer in range(block.layers):
            for r in range(0, height, 8):
                first = layer * height + r
                rows = jnp.swapaxes(x_ref[:, first : first + 8, :], 0, 1)
                v0[block.at(0, layer, HALO + r, 8), :] = rows.reshape(-1, block.breadth)
            block.set_diagonal(w, layer, NEAR, p_ref[layer * height : (layer + 1) * height, :])
        block.follow(1, [NEAR], height, v0, y1, band_ref)
        block.step(1, NEAR + REACH, inner, v0, y1, w, None, d1)
        block.follow(2, [NEAR], inner, d1, y2, band_ref)

    return call(
        kernel,
        tuple(
            jax.ShapeDtypeStruct(s, jnp.float32)
            for s in (block.shape(0), block.shape(1), block.shape(1), block.shape(2), block.diagonals())
        ),
        [IN_VMEM] * 3,
        (orbitals, potential, band),
        flops=6 * 768 * 256 * 256,
        moved=4 << 20,
    )


def left_side(block, halo, arrays, band, keep):
    v0, y1, d1, y2, w, d2, y3, out = arrays
    take_halo(block, halo, v0, w, 0)
    block.follow(1, [0], NEAR, v0, y1, band, exact=True)
    block.step(1, NEAR, REACH, v0, y1, w, None, d1)
    block.follow(2, [REACH], REACH, d1, y2, band)
    block.step(1, 0, NEAR, v0, y1, w, None, d1, (NEAR, keep))
    block.follow(2, [0], REACH, d1, y2, band)
    block.step(2, NEAR, REACH, d1, y2, w, v0, d2)
    block.step(2, REACH, REACH, d1, y2, w, v0, d2)
    block.follow(3, [0], NEAR, d2, y3, band)
    block.step(2, 0, REACH, d1, y2, w, v0, d2, (REACH, keep))
    block.step(3, 0, REACH, d2, y3, w, d1, out)


def right_side(block, halo, arrays, band, keep):
    v0, y1, d1, y2, w, d2, y3, out = arrays
    height = block.height
    take_halo(block, halo, v0, w, height)
    block.follow(1, [NEAR + height], NEAR, v0, y1, band, exact=True)
    block.step(1, NEAR + height - REACH, REACH, v0, y1, w, None, d1)
    block.follow(2, [height], REACH, d1, y2, band)
    block.step(1, NEAR + height, NEAR, v0, y1, w, None, d1, (NEAR, keep))
    block.follow(2, [height + REACH], REACH, d1, y2, band)
    block.step(2, height - REACH, REACH, d1, y2, w, v0, d2)
    block.step(2, height, REACH, d1, y2, w, v0, d2)
    block.follow(3, [height - NEAR], NEAR, d2, y3, band)
    block.step(2, height + REACH, REACH, d1, y2, w, v0, d2, (REACH, keep))
    block.step(3, height - REACH, REACH, d2, y3, w, d1, out)


def take_halo(block, halo, v0, w, passed):
    count, layers = block.count, block.layers
    past = HALO if passed else 0
    strips = halo[layers * HALO * count : layers * (HALO * count + NEAR), :].astype(jnp.float32)
    for layer in range(layers):
        source = slice(layer * HALO * count, (layer + 1) * HALO * count)
        v0[block.at(0, layer, past + passed, HALO), :] = halo[source, :].astype(jnp.float32)
        strip = strips[layer * NEAR : (layer + 1) * NEAR]
        block.set_diagonal(w, layer, passed + (NEAR if passed else 0), strip)


def filter_call(kernel, block, arrays, extra):
    given = [a for a in arrays if not isinstance(a, jax.ShapeDtypeStruct)]
    return pl.pallas_call(
        kernel,
        out_shape=tuple(jax.ShapeDtypeStruct(a.shape, a.dtype) for a in arrays),
        in_specs=[IN_VMEM] * (len(given) + len(extra)),
        out_specs=(IN_VMEM,) * len(arrays),
        input_output_aliases={i: i for i in range(len(given))},
        compiler_params=pltpu.CompilerParams(vmem_limit_bytes=VMEM_LIMIT),
        cost_estimate=pl.CostEstimate(flops=3456 * 256 * 768, bytes_accessed=3 << 20, transcendentals=0),
    )(*given, *extra)


def filtering(prepared, before, after, wrap, band, block):
    def place():
        at = lax.axis_index("grid")
        left = (at > 0).astype(jnp.float32)
        right = (at < lax.axis_size("grid") - 1).astype(jnp.float32)
        return lax.rem(at, RUN) == 0, lax.rem(at, RUN) == RUN - 1, left, right

    def early(*refs):
        before_ref, after_ref, band_ref = refs[5:8]
        arrays = refs[8:]
        opens, closes, left, right = place()

        @pl.when(jnp.logical_not(opens))
        def _():
            left_side(block, before_ref, arrays, band_ref, left)

        @pl.when(jnp.logical_not(closes))
        def _():
            right_side(block, after_ref, arrays, band_ref, right)

    def late(*refs):
        wrap_ref, band_ref = refs[8:10]
        arrays = refs[10:]
        v0, y1, d1, y2, w, d2, y3, out = arrays
        opens, closes, left, right = place()

        @pl.when(opens)
        def _():
            left_side(block, wrap_ref, arrays, band_ref, left)

        @pl.when(closes)
        def _():
            right_side(block, wrap_ref, arrays, band_ref, right)

        block.step(3, REACH, block.height - 2 * REACH, d2, y3, w, d1, out)

    made = (
        jax.ShapeDtypeStruct(block.shape(2), jnp.float32),
        jax.ShapeDtypeStruct(block.shape(3), jnp.float32),
        jax.ShapeDtypeStruct(block.shape(3), jnp.bfloat16),
    )
    arrays = filter_call(early, block, tuple(prepared) + made, (before, after, band))
    return filter_call(late, block, arrays, (wrap, band))[-1]


def rotate(blocks, rotation, parts, per, count):
    rows, breadth = blocks.shape
    total = parts * count

    def kernel(g_ref, r_ref, out_ref):
        cells = g_ref[...].astype(jnp.float32).reshape(parts, per, count, breadth)
        turn = r_ref[...]
        outs = []
        for r in range(per):
            part = cells[:, r].reshape(total, breadth).astype(jnp.bfloat16)
            product = lax.dot_general(
                turn, part, (((0,), (0,)), ((), ())), preferred_element_type=jnp.float32
            )
            outs.append(product.reshape(parts, 1, count, breadth))
        result = jnp.concatenate(outs, axis=1).reshape(rows, breadth)
        out_ref[...] = result.astype(jnp.bfloat16)

    return call(
        kernel,
        jax.ShapeDtypeStruct((rows, breadth), jnp.bfloat16),
        [IN_VMEM, IN_VMEM],
        (blocks, rotation),
        flops=2 * total * rows * breadth,
    )


def unpack(rows, count, layers, height):
    breadth = rows.shape[1]

    def kernel(q_ref, out_hbm, held, sems):
        copies = []
        for layer in range(layers):
            for r in range(0, height, 8):
                first = layer * height + r
                group = q_ref[first * count : (first + 8) * count, :].astype(jnp.float32)
                held[layer, :, r : r + 8, :] = jnp.swapaxes(group.reshape(8, count, breadth), 0, 1)
            copy = pltpu.make_async_copy(
                held.at[layer], out_hbm.at[:, pl.ds(layer * height, height), :], sems.at[layer]
            )
            copy.start()
            copies.append(copy)
        for copy in copies:
            copy.wait()

    return call(
        kernel,
        jax.ShapeDtypeStruct((count, layers * height, breadth), jnp.float32),
        [IN_VMEM],
        (rows,),
        scratch=[
            pltpu.VMEM((layers, count, height, breadth), jnp.float32),
            pltpu.SemaphoreType.DMA((layers,)),
        ],
        out_specs=IN_HBM,
    )


def local(orbitals, potential, rotation):
    count, layers, height, breadth = orbitals.shape
    cells = layers * height
    parts = lax.axis_size("orb")
    columns = lax.axis_size("grid")
    block = Block(count, layers, height, breadth)
    band = jnp.asarray(band_matrices(breadth))
    orbitals = orbitals.reshape(count, cells, breadth)
    potential = potential.reshape(cells, breadth)
    head, tail, wrapped = pack(orbitals, potential, layers, height)
    inner = [i for i in range(columns - 1) if i % RUN != RUN - 1]
    outer = [i for i in range(columns - 1) if i % RUN == RUN - 1]
    before = lax.ppermute(tail, "grid", [(i, i + 1) for i in inner])
    after = lax.ppermute(head, "grid", [(i + 1, i) for i in inner])
    wrap = lax.ppermute(wrapped, "grid", [(i, i + 1) for i in outer] + [(i + 1, i) for i in outer])
    prepared = prepare(orbitals, potential, band, block)
    filtered = filtering(prepared, before, after, wrap, band, block)
    per = cells // parts
    filtered = filtered.reshape(parts, per * count, breadth)
    gathered = lax.all_to_all(filtered, "orb", 0, 0, tiled=True)
    rotated = rotate(gathered.reshape(cells * count, breadth), rotation, parts, per, count)
    returned = lax.all_to_all(rotated.reshape(parts, per * count, breadth), "orb", 0, 0, tiled=True)
    result = unpack(returned.reshape(cells * count, breadth), count, layers, height)
    return result.reshape(count, layers, height, breadth)


def solution(mesh):
    return jax.shard_map(
        local,
        mesh=mesh,
        in_specs=(P("orb", None, "grid", None), P(None, "grid", None), P()),
        out_specs=P("orb", None, "grid", None),
        check_vma=False,
    )
```
